32 devices in a mesh: grp: 2 (over y), wide: 4 (over z), col: 2 (over x), sub: 2 (over core).
Axes of the slice: x: 2, y: 2, z: 4, core: 2. Of those that a mesh axis runs over, the one named last changes fastest.
Arguments:
- inputs: bfloat16 [2048, 28672], P(('grp', 'col', 'sub'), 'wide'), parts along dimension 0, may hold values from -6 to 6
- targets: bfloat16 [2048, 8192], P(('grp', 'wide'), ('col', 'sub')), parts along dimension 0, may hold values from -6 to 6
- weight: bfloat16 [28672, 8192], P('wide', ('col', 'sub')), may hold values from -0.03125 to 0.03125
- factor_in: bfloat16 [16, 28672], P('grp', 'wide'), parts along dimension 0, may hold values from -4 to 4
- factor_out: bfloat16 [16, 8192], P('grp', ('col', 'sub')), parts along dimension 0, may hold values from -4 to 4
Outputs:
- outputs: bfloat16 [2048, 8192], P(('grp', 'wide'), ('col', 'sub')), parts along dimension 0
- weight_step: bfloat16 [57344, 8192], P(('grp', 'wide'), ('col', 'sub')), parts along dimension 0
The draws below stay inside these ranges and needn't reach their ends.
There are 2 independent parts, one for each index of `grp`. The reference program is written for one: setup_inputs(seed, part) draws one part's arguments, and reference() takes and returns one part's arrays. A program takes and returns all parts, laid end to end along the dimension named above; an argument that names none is the same for every part. Nothing has to cross between parts.
All inputs are finite; a program needn't handle non-finite values.
Results may differ from the reference program's by a relative error of at most 0.001.
Values may be sent and summed in bfloat16 or wider, within the bound.
A program may use at most 192 MiB of HBM per device.

```python
import math
import jax
import jax.numpy as jnp
from jax import lax

D = 8192
FF = 28672
MEMBERS = 8
SEQ = 128
ROWS = 1024


def level_of(key, extent, pieces, low, largest):
    def one(position, shards_of):
        heights = jax.random.uniform(jax.random.fold_in(jax.random.fold_in(key, 6), position), (shards_of,), jnp.float32, low / len(pieces), largest / len(pieces))
        return jnp.repeat(jnp.exp(heights), extent[position] // shards_of).reshape((-1,) + (1,) * (len(extent) - position - 1))

    level = one(*pieces[0])
    for cut in pieces[1:]:
        level = level * one(*cut)
    return level


def scatter_about(rng, dims, scale, most, pieces=(), kind=jnp.bfloat16):
    drawn = scale * jax.random.normal(rng, dims, jnp.float32)
    if pieces:
        drawn = drawn * level_of(rng, dims, pieces, -0.22, 0.18)
    return jnp.clip(drawn, -most, most).astype(kind)


def setup_inputs(seed: int = 0, part: int = 0) -> dict:
    key_of = jax.random.split(jax.random.key(seed), 6)
    part_splits = jax.random.split(jax.random.fold_in(key_of[5], part), 6)
    return {
        "inputs": scatter_about(part_splits[0], (ROWS, FF), 1.0, 6.0, ((0, 4), (1, 4))),
        "targets": scatter_about(part_splits[1], (ROWS, D), 1.0, 6.0, ((0, 4), (1, 4))),
        "weight": scatter_about(key_of[2], (FF, D), FF ** -0.5, 0.03125, ((0, 4), (1, 4))),
        "factor_in": scatter_about(part_splits[3], (MEMBERS, FF), 1.0, 4.0, ((1, 4),)),
        "factor_out": scatter_about(part_splits[4], (MEMBERS, D), 1.0, 4.0, ((1, 4),)),
    }


noise_scale = 1.0

def reference(inputs, targets, weight, factor_in, factor_out):
    base = jnp.dot(inputs, weight, preferred_element_type=jnp.float32)
    shaped = inputs.astype(jnp.float32).reshape(MEMBERS, SEQ, FF)
    projected = jnp.einsum('msf,mf->ms', shaped, factor_in.astype(jnp.float32)).reshape(MEMBERS * SEQ)
    expanded = jnp.repeat(factor_out.astype(jnp.float32), SEQ, axis=0)
    perturbed = base + noise_scale * (projected / math.sqrt(FF))[:, None] * expanded
    outputs = perturbed.astype(jnp.bfloat16)
    errors = perturbed - targets.astype(jnp.float32)
    loss = lax.optimization_barrier(jnp.sum((errors * errors).reshape(MEMBERS, SEQ * D), axis=1)) / (SEQ * D)
    fitness = jnp.mean(loss) - loss
    scaled = factor_in.astype(jnp.float32) * fitness[:, None]
    weight_step = jnp.dot(scaled.T, factor_out.astype(jnp.float32), precision=lax.Precision.HIGHEST) / noise_scale
    return (outputs, weight_step.astype(jnp.bfloat16))
```

```python
import math

import jax
import jax.numpy as jnp
from jax import lax
from jax.sharding import PartitionSpec as P

D = 8192
FF = 28672
MEMBERS = 8
SEQ = 128
PIECES = 4
SPAN = 250.0
FLOOR = -124.0


noise_scale = 1.0


def encode(rows):
    top = jnp.max(jnp.abs(rows), axis=-1, keepdims=True)
    scale = lax.reduce_precision(jnp.maximum(top, 1e-30) * 1.01, 8, 7)
    height = jnp.exp2(jnp.abs(rows) * (SPAN / scale) + FLOOR)
    code = jnp.where(rows < 0, -height, height).astype(jnp.bfloat16)
    side = jnp.broadcast_to(scale, rows.shape[:-1] + (128,)).astype(jnp.bfloat16)
    return jnp.concatenate([code, side], axis=-1)


def decode(message):
    code = message[..., :-128].astype(jnp.float32)
    scale = message[..., -128:-127].astype(jnp.float32)
    size = (jnp.log2(jnp.abs(code)) - FLOOR) * (scale / SPAN)
    return jnp.where(code < 0, -size, size)


def exchanged(block, axis, bit):
    route = [(i, i ^ bit) for i in range(lax.axis_size(axis))]
    return lax.ppermute(block, axis, route)


def piece_product(gathered, weight, factor_in, factor_out, first_row, blocks, height, local_rows):
    members = [(b * local_rows + first_row) // SEQ for b in range(blocks)]
    fi = jnp.stack([factor_in[m] for m in members])
    fo = jnp.stack([factor_out[m] for m in members]).astype(jnp.float32)
    shaped = gathered.reshape(blocks, height, gathered.shape[1])
    projected = jnp.einsum("bhf,bf->bh", shaped, fi, preferred_element_type=jnp.float32)
    product = jnp.dot(gathered, weight, preferred_element_type=jnp.float32)
    product = product.reshape(blocks, height, weight.shape[1])
    factor_scale = noise_scale / math.sqrt(FF)
    return product + factor_scale * projected[:, :, None] * fo[:, None, :]


def reduce_scattered(product, me):
    held = product
    cycle = lax.axis_size("wide")
    bit = 1
    while bit < cycle:
        held = held.reshape((held.shape[0] // 2, 2) + held.shape[1:])
        mine = (me // bit) % 2
        sent = lax.dynamic_index_in_dim(held, 1 - mine, 1, keepdims=False)
        kept = lax.dynamic_index_in_dim(held, mine, 1, keepdims=False)
        held = kept + decode(exchanged(encode(sent), "wide", bit))
        bit *= 2
    return held[0]


def per_device(inputs, targets, weight, factor_in, factor_out):
    cycle = lax.axis_size("wide")
    local_rows = targets.shape[0]
    me = lax.axis_index("wide")
    per_shard = inputs.shape[0] // local_rows
    height = local_rows // PIECES
    shaped = inputs.reshape(per_shard, PIECES, height, inputs.shape[1])

    sums = []
    for j in range(PIECES):
        own = shaped[:, j].reshape(per_shard * height, inputs.shape[1])
        gathered = lax.all_gather(own, ("col", "sub"), axis=0, tiled=True)
        product = piece_product(
            gathered, weight, factor_in, factor_out, j * height, cycle, height, local_rows
        )
        sums.append(reduce_scattered(product, me))
    perturbed = jnp.concatenate(sums, axis=0)
    outputs = perturbed.astype(jnp.bfloat16)
    errors = perturbed - targets.astype(jnp.float32)
    row_sums = jnp.sum(errors * errors, axis=1)
    row_index = me * local_rows + jnp.arange(local_rows, dtype=jnp.int32)
    member_of = row_index // SEQ
    onehot = (member_of[:, None] == jnp.arange(MEMBERS, dtype=jnp.int32)[None, :]).astype(
        jnp.float32
    )
    partial_loss = jnp.sum(onehot * row_sums[:, None], axis=0)
    loss = lax.psum(partial_loss, ("wide", "col", "sub")) / (SEQ * D)
    fitness = jnp.mean(loss) - loss
    side = factor_out.astype(jnp.float32) * fitness[:, None]
    high = lax.reduce_precision(side, 8, 7)
    rest = side - high
    middle = lax.reduce_precision(rest, 8, 7)
    low = rest - middle
    right = jnp.concatenate([high, middle, low], axis=0).astype(jnp.bfloat16)
    left = jnp.concatenate([factor_in] * 3, axis=0)
    weight_step = (
        lax.dot_general(
            left, right, (((0,), (0,)), ((), ())), preferred_element_type=jnp.float32
        )
        / noise_scale
    )
    return (outputs, weight_step.astype(jnp.bfloat16))


def solution(mesh):
    placed = (
        P(("grp", "col", "sub"), "wide"),
        P(("grp", "wide"), ("col", "sub")),
        P("wide", ("col", "sub")),
        P("grp", "wide"),
        P("grp", ("col", "sub")),
    )
    return jax.shard_map(
        per_device,
        mesh=mesh,
        in_specs=placed,
        out_specs=(P(("grp", "wide"), ("col", "sub")), P(("grp", "wide"), ("col", "sub"))),
        check_vma=False,
    )
```

```python
import math

import jax
import jax.numpy as jnp
from jax import lax
from jax.sharding import PartitionSpec as P

D = 8192
FF = 28672
MEMBERS = 8
SEQ = 128
PIECES = 4
SPAN = 250.0
FLOOR = -124.0


noise_scale = 1.0


def encode(rows):
    top = jnp.max(jnp.abs(rows), axis=-1, keepdims=True)
    scale = lax.reduce_precision(jnp.maximum(top, 1e-30) * 1.01, 8, 7)
    height = jnp.exp2(jnp.abs(rows) * (SPAN / scale) + FLOOR)
    code = jnp.where(rows < 0, -height, height).astype(jnp.bfloat16)
    side = jnp.broadcast_to(scale, rows.shape[:-1] + (128,)).astype(jnp.bfloat16)
    return jnp.concatenate([code, side], axis=-1)


def decode(message):
    code = message[..., :-128].astype(jnp.float32)
    scale = message[..., -128:-127].astype(jnp.float32)
    size = (jnp.log2(jnp.abs(code)) - FLOOR) * (scale / SPAN)
    return jnp.where(code < 0, -size, size)


def exchanged(block, axis, bit):
    route = [(i, i ^ bit) for i in range(lax.axis_size(axis))]
    return lax.ppermute(block, axis, route)


def bits_of(size):
    return [1 << k for k in range(size.bit_length() - 1)]


def spread(block):
    held = [block]
    for axis in ("col", "sub"):
        for bit in reversed(bits_of(lax.axis_size(axis))):
            held = [part for b in held for part in (b, exchanged(b, axis, bit))]
    return held


def piece_product(rows, weight, factor_in, factor_out, members, height):
    blocks = rows.shape[0] // height
    fi = jnp.take(factor_in, members, axis=0)
    fo = jnp.take(factor_out, members, axis=0).astype(jnp.float32)
    shaped = rows.reshape(blocks, height, rows.shape[1])
    projected = jnp.einsum("bhf,bf->bh", shaped, fi, preferred_element_type=jnp.float32)
    product = jnp.dot(rows, weight, preferred_element_type=jnp.float32)
    product = product.reshape(blocks, height, weight.shape[1])
    factor_scale = noise_scale / math.sqrt(FF)
    return product + factor_scale * projected[:, :, None] * fo[:, None, :]


def halves(held, bit, me, flip):
    held = held.reshape((held.shape[0] // 2, 2) + held.shape[1:])
    mine = ((me // bit) % 2) ^ ((flip // bit) % 2)
    sent = lax.dynamic_index_in_dim(held, 1 - mine, 1, keepdims=False)
    kept = lax.dynamic_index_in_dim(held, mine, 1, keepdims=False)
    return encode(sent), kept


def per_device(inputs, targets, weight, factor_in, factor_out):
    cycle = lax.axis_size("wide")
    local_rows = targets.shape[0]
    me = lax.axis_index("wide")
    shard = lax.axis_index("col") * lax.axis_size("sub") + lax.axis_index("sub")
    per_shard = inputs.shape[0] // local_rows
    height = local_rows // PIECES
    shaped = inputs.reshape(per_shard, PIECES, height, inputs.shape[1])
    flip = shard * per_shard
    order = jnp.arange(cycle, dtype=jnp.int32) ^ flip

    parts = [
        spread(shaped[:, j].reshape(per_shard * height, inputs.shape[1])) for j in range(PIECES)
    ]
    stages = bits_of(cycle)
    held = [None] * PIECES
    pending = [None] * PIECES
    after = []
    for turn in range(PIECES + len(stages)):
        made = []
        if turn < PIECES:
            ready, _ = lax.optimization_barrier((parts[turn], after))
            members = (order * local_rows + turn * height) // SEQ
            product = piece_product(
                jnp.concatenate(ready, axis=0), weight, factor_in, factor_out, members, height
            )
            pending[turn] = halves(product, stages[0], me, flip)
            made.append(pending[turn][0])
        for j in range(min(turn, PIECES)):
            stage = turn - j - 1
            if stage >= len(stages):
                continue
            message, kept = pending[j]
            held[j] = kept + decode(exchanged(message, "wide", stages[stage]))
            if stage + 1 < len(stages):
                pending[j] = halves(held[j], stages[stage + 1], me, flip)
                made.append(pending[j][0])
        after = made
    sums = [h[0] for h in held]
    perturbed = jnp.concatenate(sums, axis=0)
    outputs = perturbed.astype(jnp.bfloat16)
    errors = perturbed - targets.astype(jnp.float32)
    row_sums = jnp.sum(errors * errors, axis=1)
    row_index = me * local_rows + jnp.arange(local_rows, dtype=jnp.int32)
    member_of = row_index // SEQ
    onehot = (member_of[:, None] == jnp.arange(MEMBERS, dtype=jnp.int32)[None, :]).astype(
        jnp.float32
    )
    partial_loss = jnp.sum(onehot * row_sums[:, None], axis=0)
    for axis in ("sub", "col", "wide"):
        for bit in bits_of(lax.axis_size(axis)):
            partial_loss = partial_loss + exchanged(partial_loss, axis, bit)
    loss = partial_loss / (SEQ * D)
    fitness = jnp.mean(loss) - loss
    side = factor_out.astype(jnp.float32) * fitness[:, None]
    high = lax.reduce_precision(side, 8, 7)
    rest = side - high
    middle = lax.reduce_precision(rest, 8, 7)
    low = rest - middle
    right = jnp.concatenate([high, middle, low], axis=0).astype(jnp.bfloat16)
    left = jnp.concatenate([factor_in] * 3, axis=0)
    weight_step = (
        lax.dot_general(
            left, right, (((0,), (0,)), ((), ())), preferred_element_type=jnp.float32
        )
        / noise_scale
    )
    return (outputs, weight_step.astype(jnp.bfloat16))


def solution(mesh):
    placed = (
        P(("grp", "col", "sub"), "wide"),
        P(("grp", "wide"), ("col", "sub")),
        P("wide", ("col", "sub")),
        P("grp", "wide"),
        P("grp", ("col", "sub")),
    )
    return jax.shard_map(
        per_device,
        mesh=mesh,
        in_specs=placed,
        out_specs=(P(("grp", "wide"), ("col", "sub")), P(("grp", "wide"), ("col", "sub"))),
        check_vma=False,
    )
```

```python
import math

import jax
import jax.numpy as jnp
from jax import lax
from jax.sharding import PartitionSpec as P

D = 8192
FF = 28672
MEMBERS = 8
SEQ = 128
SHARES = (2, 2, 2, 2)
SPAN = 250.0
FLOOR = -124.0


noise_scale = 1.0


def encode(rows):
    top = jnp.max(jnp.abs(rows), axis=-1, keepdims=True)
    scale = lax.reduce_precision(jnp.maximum(top, 1e-30) * 1.01, 8, 7)
    height = jnp.exp2(jnp.abs(rows) * (SPAN / scale) + FLOOR)
    code = jnp.where(rows < 0, -height, height).astype(jnp.bfloat16)
    side = jnp.broadcast_to(scale, rows.shape[:-1] + (128,)).astype(jnp.bfloat16)
    return jnp.concatenate([code, side], axis=-1)


def decode(message):
    code = message[..., :-128].astype(jnp.float32)
    scale = message[..., -128:-127].astype(jnp.float32)
    size = (jnp.log2(jnp.abs(code)) - FLOOR) * (scale / SPAN)
    return jnp.where(code < 0, -size, size)


def exchanged(block, axis, bit):
    route = [(i, i ^ bit) for i in range(lax.axis_size(axis))]
    return lax.ppermute(block, axis, route)


def bits_of(size):
    return [1 << k for k in range(size.bit_length() - 1)]


def crossed(block, axis):
    held = block if isinstance(block, list) else [block]
    for bit in reversed(bits_of(lax.axis_size(axis))):
        held = [part for b in held for part in (b, exchanged(b, axis, bit))]
    return held


def piece_product(rows, weight, projected, fo):
    blocks, units, height = projected.shape
    product = jnp.dot(rows, weight, preferred_element_type=jnp.float32)
    product = product.reshape(blocks, units, height, weight.shape[1])
    factor_scale = noise_scale / math.sqrt(FF)
    product = product + factor_scale * projected[..., None] * fo[:, :, None, :]
    return product.reshape(blocks, units * height, weight.shape[1])


def halves(held, bit, me, flip):
    held = held.reshape((held.shape[0] // 2, 2) + held.shape[1:])
    mine = ((me // bit) % 2) ^ ((flip // bit) % 2)
    sent = lax.dynamic_index_in_dim(held, 1 - mine, 1, keepdims=False)
    kept = lax.dynamic_index_in_dim(held, mine, 1, keepdims=False)
    return encode(sent), kept


def per_device(inputs, targets, weight, factor_in, factor_out):
    cycle = lax.axis_size("wide")
    local_rows = targets.shape[0]
    me = lax.axis_index("wide")
    shard = lax.axis_index("col") * lax.axis_size("sub") + lax.axis_index("sub")
    per_shard = inputs.shape[0] // local_rows
    total_units = sum(SHARES)
    height = local_rows // total_units
    units = jnp.arange(total_units, dtype=jnp.int32) * height
    flip = shard * per_shard
    order = jnp.arange(cycle, dtype=jnp.int32) ^ flip

    own_blocks = flip + jnp.arange(per_shard, dtype=jnp.int32)
    own_members = (own_blocks[:, None] * local_rows + units[None, :]) // SEQ
    own_projected = jnp.einsum(
        "buhf,buf->buh",
        inputs.reshape(per_shard, total_units, height, inputs.shape[1]),
        jnp.take(factor_in, own_members, axis=0),
        preferred_element_type=jnp.float32,
    )
    projected = jnp.concatenate(crossed(crossed(own_projected, "col"), "sub"), axis=0)
    members = (order[:, None] * local_rows + units[None, :]) // SEQ
    expanded = jnp.take(factor_out, members, axis=0).astype(jnp.float32)

    shaped = inputs.reshape(per_shard, local_rows, inputs.shape[1])
    firsts = [sum(SHARES[:j]) for j in range(len(SHARES))]
    parts, arrived = [], []
    for first, share in zip(firsts, SHARES):
        own = shaped[:, first * height : (first + share) * height].reshape(-1, inputs.shape[1])
        gate = []
        if len(arrived) == 1:
            gate = arrived[0]
        elif arrived:
            gate = parts[-2]
        own, _ = lax.optimization_barrier((own, gate))
        arrived.append(crossed(own, "col"))
        parts.append(crossed(arrived[-1], "sub"))
    stages = bits_of(cycle)
    pieces = len(SHARES)
    held = [None] * pieces
    pending = [None] * pieces
    after = []
    for turn in range(pieces + len(stages)):
        made = []
        if turn < pieces:
            ready, _ = lax.optimization_barrier((parts[turn], after))
            span = slice(firsts[turn], firsts[turn] + SHARES[turn])
            product = piece_product(
                jnp.concatenate(ready, axis=0), weight, projected[:, span], expanded[:, span]
            )
            pending[turn] = halves(product, stages[0], me, flip)
            made.append(pending[turn][0])
        for j in range(min(turn, pieces)):
            stage = turn - j - 1
            if stage >= len(stages):
                continue
            message, kept = pending[j]
            held[j] = kept + decode(exchanged(message, "wide", stages[stage]))
            if stage + 1 < len(stages):
                pending[j] = halves(held[j], stages[stage + 1], me, flip)
                made.append(pending[j][0])
        after = made
    sums = [h[0] for h in held]
    perturbed = jnp.concatenate(sums, axis=0)
    outputs = perturbed.astype(jnp.bfloat16)
    errors = perturbed - targets.astype(jnp.float32)
    row_sums = jnp.sum(errors * errors, axis=1)
    row_index = me * local_rows + jnp.arange(local_rows, dtype=jnp.int32)
    member_of = row_index // SEQ
    onehot = (member_of[:, None] == jnp.arange(MEMBERS, dtype=jnp.int32)[None, :]).astype(
        jnp.float32
    )
    partial_loss = jnp.sum(onehot * row_sums[:, None], axis=0)
    for axis in ("sub", "col", "wide"):
        for bit in bits_of(lax.axis_size(axis)):
            partial_loss = partial_loss + exchanged(partial_loss, axis, bit)
    loss = partial_loss / (SEQ * D)
    fitness = jnp.mean(loss) - loss
    side = factor_out.astype(jnp.float32) * fitness[:, None]
    high = lax.reduce_precision(side, 8, 7)
    rest = side - high
    middle = lax.reduce_precision(rest, 8, 7)
    low = rest - middle
    right = jnp.concatenate([high, middle, low], axis=0).astype(jnp.bfloat16)
    left = jnp.concatenate([factor_in] * 3, axis=0)
    weight_step = (
        lax.dot_general(
            left, right, (((0,), (0,)), ((), ())), preferred_element_type=jnp.float32
        )
        / noise_scale
    )
    return (outputs, weight_step.astype(jnp.bfloat16))


def solution(mesh):
    placed = (
        P(("grp", "col", "sub"), "wide"),
        P(("grp", "wide"), ("col", "sub")),
        P("wide", ("col", "sub")),
        P("grp", "wide"),
        P("grp", ("col", "sub")),
    )
    return jax.shard_map(
        per_device,
        mesh=mesh,
        in_specs=placed,
        out_specs=(P(("grp", "wide"), ("col", "sub")), P(("grp", "wide"), ("col", "sub"))),
        check_vma=False,
    )
```

```python
import math

import jax
import jax.numpy as jnp
from jax import lax
from jax.sharding import PartitionSpec as P

D = 8192
FF = 28672
MEMBERS = 8
SEQ = 128
SHARES = (2, 3, 2, 1)
SPAN = 250.0
FLOOR = -124.0


noise_scale = 1.0


def encode(rows):
    top = jnp.max(jnp.abs(rows), axis=-1, keepdims=True)
    scale = lax.reduce_precision(jnp.maximum(top, 1e-30) * 1.01, 8, 7)
    height = jnp.exp2(jnp.abs(rows) * (SPAN / scale) + FLOOR)
    code = jnp.where(rows < 0, -height, height).astype(jnp.bfloat16)
    side = jnp.broadcast_to(scale, rows.shape[:-1] + (128,)).astype(jnp.bfloat16)
    return jnp.concatenate([code, side], axis=-1)


def decode(message):
    code = message[..., :-128].astype(jnp.float32)
    scale = message[..., -128:-127].astype(jnp.float32)
    size = (jnp.log2(jnp.abs(code)) - FLOOR) * (scale / SPAN)
    return jnp.where(code < 0, -size, size)


def exchanged(block, axis, bit):
    route = [(i, i ^ bit) for i in range(lax.axis_size(axis))]
    return lax.ppermute(block, axis, route)


def bits_of(size):
    return [1 << k for k in range(size.bit_length() - 1)]


def crossed(block, axis):
    held = block if isinstance(block, list) else [block]
    for bit in reversed(bits_of(lax.axis_size(axis))):
        held = [part for b in held for part in (b, exchanged(b, axis, bit))]
    return held


def piece_product(rows, weight, projected, fo):
    blocks, units, height = projected.shape
    product = jnp.dot(rows, weight, preferred_element_type=jnp.float32)
    product = product.reshape(blocks, units, height, weight.shape[1])
    factor_scale = noise_scale / math.sqrt(FF)
    product = product + factor_scale * projected[..., None] * fo[:, :, None, :]
    return product.reshape(blocks, units * height, weight.shape[1])


def halves(held, bit, me, flip):
    held = held.reshape((held.shape[0] // 2, 2) + held.shape[1:])
    mine = ((me // bit) % 2) ^ ((flip // bit) % 2)
    sent = lax.dynamic_index_in_dim(held, 1 - mine, 1, keepdims=False)
    kept = lax.dynamic_index_in_dim(held, mine, 1, keepdims=False)
    return encode(sent), kept


def per_device(inputs, targets, weight, factor_in, factor_out):
    cycle = lax.axis_size("wide")
    local_rows = targets.shape[0]
    me = lax.axis_index("wide")
    shard = lax.axis_index("col") * lax.axis_size("sub") + lax.axis_index("sub")
    per_shard = inputs.shape[0] // local_rows
    total_units = sum(SHARES)
    height = local_rows // total_units
    units = jnp.arange(total_units, dtype=jnp.int32) * height
    flip = shard * per_shard
    order = jnp.arange(cycle, dtype=jnp.int32) ^ flip

    own_blocks = flip + jnp.arange(per_shard, dtype=jnp.int32)
    own_members = (own_blocks[:, None] * local_rows + units[None, :]) // SEQ
    own_projected = jnp.einsum(
        "buhf,buf->buh",
        inputs.reshape(per_shard, total_units, height, inputs.shape[1]),
        jnp.take(factor_in, own_members, axis=0),
        preferred_element_type=jnp.float32,
    )
    projected = jnp.concatenate(crossed(crossed(own_projected, "col"), "sub"), axis=0)
    members = (order[:, None] * local_rows + units[None, :]) // SEQ
    expanded = jnp.take(factor_out, members, axis=0).astype(jnp.float32)

    shaped = inputs.reshape(per_shard, local_rows, inputs.shape[1])
    firsts = [sum(SHARES[:j]) for j in range(len(SHARES))]
    parts, arrived = [], []
    for first, share in zip(firsts, SHARES):
        own = shaped[:, first * height : (first + share) * height].reshape(-1, inputs.shape[1])
        gate = []
        if len(arrived) == 1:
            gate = arrived[0]
        elif arrived:
            gate = parts[-2]
        own, _ = lax.optimization_barrier((own, gate))
        arrived.append(crossed(own, "col"))
        parts.append(crossed(arrived[-1], "sub"))
    stages = bits_of(cycle)
    pieces = len(SHARES)
    held = [None] * pieces
    pending = [None] * pieces
    after = []
    for turn in range(pieces + len(stages)):
        made = []
        if turn < pieces:
            ready, _ = lax.optimization_barrier((parts[turn], after))
            span = slice(firsts[turn], firsts[turn] + SHARES[turn])
            product = piece_product(
                jnp.concatenate(ready, axis=0), weight, projected[:, span], expanded[:, span]
            )
            pending[turn] = halves(product, stages[0], me, flip)
            made.append(pending[turn][0])
        for j in range(min(turn, pieces)):
            stage = turn - j - 1
            if stage >= len(stages):
                continue
            message, kept = pending[j]
            received = exchanged(message, "wide", stages[stage])
            if turn < pieces:
                received, _ = lax.optimization_barrier((received, made[0]))
            held[j] = kept + decode(received)
            if stage + 1 < len(stages):
                pending[j] = halves(held[j], stages[stage + 1], me, flip)
                made.append(pending[j][0])
        after = made[:1]
    sums = [h[0] for h in held]
    perturbed = jnp.concatenate(sums, axis=0)
    outputs = perturbed.astype(jnp.bfloat16)
    errors = perturbed - targets.astype(jnp.float32)
    row_sums = jnp.sum(errors * errors, axis=1)
    row_index = me * local_rows + jnp.arange(local_rows, dtype=jnp.int32)
    member_of = row_index // SEQ
    onehot = (member_of[:, None] == jnp.arange(MEMBERS, dtype=jnp.int32)[None, :]).astype(
        jnp.float32
    )
    partial_loss = jnp.sum(onehot * row_sums[:, None], axis=0)
    for axis in ("sub", "col", "wide"):
        for bit in bits_of(lax.axis_size(axis)):
            partial_loss = partial_loss + exchanged(partial_loss, axis, bit)
    loss = partial_loss / (SEQ * D)
    fitness = jnp.mean(loss) - loss
    side = factor_out.astype(jnp.float32) * fitness[:, None]
    high = lax.reduce_precision(side, 8, 7)
    rest = side - high
    middle = lax.reduce_precision(rest, 8, 7)
    low = rest - middle
    right = jnp.concatenate([high, middle, low], axis=0).astype(jnp.bfloat16)
    left = jnp.concatenate([factor_in] * 3, axis=0)
    weight_step = (
        lax.dot_general(
            left, right, (((0,), (0,)), ((), ())), preferred_element_type=jnp.float32
        )
        / noise_scale
    )
    return (outputs, weight_step.astype(jnp.bfloat16))


def solution(mesh):
    placed = (
        P(("grp", "col", "sub"), "wide"),
        P(("grp", "wide"), ("col", "sub")),
        P("wide", ("col", "sub")),
        P("grp", "wide"),
        P("grp", ("col", "sub")),
    )
    return jax.shard_map(
        per_device,
        mesh=mesh,
        in_specs=placed,
        out_specs=(P(("grp", "wide"), ("col", "sub")), P(("grp", "wide"), ("col", "sub"))),
        check_vma=False,
    )
```

```python
import math

import jax
import jax.numpy as jnp
from jax import lax
from jax.sharding import PartitionSpec as P

D = 8192
FF = 28672
MEMBERS = 8
SEQ = 128
SHARES = (2, 2, 2, 2)
SPAN = 250.0
FLOOR = -124.0


noise_scale = 1.0


def encode(rows):
    top = jnp.max(jnp.abs(rows), axis=-1, keepdims=True)
    scale = lax.reduce_precision(jnp.maximum(top, 1e-30) * 1.01, 8, 7)
    height = jnp.exp2(jnp.abs(rows) * (SPAN / scale) + FLOOR)
    code = jnp.where(rows < 0, -height, height).astype(jnp.bfloat16)
    side = jnp.broadcast_to(scale, rows.shape[:-1] + (128,)).astype(jnp.bfloat16)
    return jnp.concatenate([code, side], axis=-1)


def decode(message):
    code = message[..., :-128].astype(jnp.float32)
    scale = message[..., -128:-127].astype(jnp.float32)
    size = (jnp.log2(jnp.abs(code)) - FLOOR) * (scale / SPAN)
    return jnp.where(code < 0, -size, size)


def exchanged(block, axis, bit):
    route = [(i, i ^ bit) for i in range(lax.axis_size(axis))]
    return lax.ppermute(block, axis, route)


def bits_of(size):
    return [1 << k for k in range(size.bit_length() - 1)]


def crossed(block, axis):
    held = block if isinstance(block, list) else [block]
    for bit in reversed(bits_of(lax.axis_size(axis))):
        held = [part for b in held for part in (b, exchanged(b, axis, bit))]
    return held


def piece_product(rows, weight, projected, fo):
    blocks, units, height = projected.shape
    product = jnp.dot(rows, weight, preferred_element_type=jnp.float32)
    product = product.reshape(blocks, units, height, weight.shape[1])
    factor_scale = noise_scale / math.sqrt(FF)
    product = product + factor_scale * projected[..., None] * fo[:, :, None, :]
    return product.reshape(blocks, units * height, weight.shape[1])


def halves(held, bit, me, flip):
    held = held.reshape((held.shape[0] // 2, 2) + held.shape[1:])
    mine = ((me // bit) % 2) ^ ((flip // bit) % 2)
    sent = lax.dynamic_index_in_dim(held, 1 - mine, 1, keepdims=False)
    kept = lax.dynamic_index_in_dim(held, mine, 1, keepdims=False)
    return encode(sent), kept


def per_device(inputs, targets, weight, factor_in, factor_out):
    cycle = lax.axis_size("wide")
    local_rows = targets.shape[0]
    me = lax.axis_index("wide")
    shard = lax.axis_index("col") * lax.axis_size("sub") + lax.axis_index("sub")
    per_shard = inputs.shape[0] // local_rows
    total_units = sum(SHARES)
    height = local_rows // total_units
    units = jnp.arange(total_units, dtype=jnp.int32) * height
    flip = shard * per_shard
    order = jnp.arange(cycle, dtype=jnp.int32) ^ flip

    own_blocks = flip + jnp.arange(per_shard, dtype=jnp.int32)
    own_members = (own_blocks[:, None] * local_rows + units[None, :]) // SEQ
    own_projected = jnp.einsum(
        "buhf,buf->buh",
        inputs.reshape(per_shard, total_units, height, inputs.shape[1]),
        jnp.take(factor_in, own_members, axis=0),
        preferred_element_type=jnp.float32,
    )
    projected = jnp.concatenate(crossed(crossed(own_projected, "col"), "sub"), axis=0)
    members = (order[:, None] * local_rows + units[None, :]) // SEQ
    expanded = jnp.take(factor_out, members, axis=0).astype(jnp.float32)

    shaped = inputs.reshape(per_shard, local_rows, inputs.shape[1])
    firsts = [sum(SHARES[:j]) for j in range(len(SHARES))]
    parts, arrived = [], []
    for first, share in zip(firsts, SHARES):
        own = shaped[:, first * height : (first + share) * height].reshape(-1, inputs.shape[1])
        gate = []
        if len(arrived) == 1:
            gate = arrived[0]
        elif arrived:
            gate = parts[-2]
        own, _ = lax.optimization_barrier((own, gate))
        arrived.append(crossed(own, "col"))
        parts.append(crossed(arrived[-1], "sub"))
    stages = bits_of(cycle)
    pieces = len(SHARES)
    held = [None] * pieces
    pending = [None] * pieces
    after = []
    for turn in range(pieces + len(stages)):
        made = []
        if turn < pieces:
            ready, _ = lax.optimization_barrier((parts[turn], after))
            span = slice(firsts[turn], firsts[turn] + SHARES[turn])
            product = piece_product(
                jnp.concatenate(ready, axis=0), weight, projected[:, span], expanded[:, span]
            )
            pending[turn] = halves(product, stages[0], me, flip)
            made.append(pending[turn][0])
        for j in range(min(turn, pieces)):
            stage = turn - j - 1
            if stage >= len(stages):
                continue
            message, kept = pending[j]
            received = exchanged(message, "wide", stages[stage])
            if turn < pieces:
                received, _ = lax.optimization_barrier((received, made[0]))
            held[j] = kept + decode(received)
            if stage + 1 < len(stages):
                pending[j] = halves(held[j], stages[stage + 1], me, flip)
                made.append(pending[j][0])
        after = made[:1]
    sums = [h[0] for h in held]
    perturbed = jnp.concatenate(sums, axis=0)
    outputs = perturbed.astype(jnp.bfloat16)
    errors = perturbed - targets.astype(jnp.float32)
    row_sums = jnp.sum(errors * errors, axis=1)
    row_index = me * local_rows + jnp.arange(local_rows, dtype=jnp.int32)
    member_of = row_index // SEQ
    onehot = (member_of[:, None] == jnp.arange(MEMBERS, dtype=jnp.int32)[None, :]).astype(
        jnp.float32
    )
    partial_loss = jnp.sum(onehot * row_sums[:, None], axis=0)
    for axis in ("sub", "col", "wide"):
        for bit in bits_of(lax.axis_size(axis)):
            partial_loss = partial_loss + exchanged(partial_loss, axis, bit)
    loss = partial_loss / (SEQ * D)
    fitness = jnp.mean(loss) - loss
    side = factor_out.astype(jnp.float32) * fitness[:, None]
    high = lax.reduce_precision(side, 8, 7)
    rest = side - high
    middle = lax.reduce_precision(rest, 8, 7)
    low = rest - middle
    right = jnp.concatenate([high, middle, low], axis=0).astype(jnp.bfloat16)
    left = jnp.concatenate([factor_in] * 3, axis=0)
    weight_step = (
        lax.dot_general(
            left, right, (((0,), (0,)), ((), ())), preferred_element_type=jnp.float32
        )
        / noise_scale
    )
    return (outputs, weight_step.astype(jnp.bfloat16))


def solution(mesh):
    placed = (
        P(("grp", "col", "sub"), "wide"),
        P(("grp", "wide"), ("col", "sub")),
        P("wide", ("col", "sub")),
        P("grp", "wide"),
        P("grp", ("col", "sub")),
    )
    return jax.shard_map(
        per_device,
        mesh=mesh,
        in_specs=placed,
        out_specs=(P(("grp", "wide"), ("col", "sub")), P(("grp", "wide"), ("col", "sub"))),
        check_vma=False,
    )
```
